512 devices in a mesh: grp: 8 (over y), slot: 64 (over x, z, core).
Axes of the slice: x: 4, y: 8, z: 8, core: 2. Of those that a mesh axis runs over, the one named last changes fastest.
Arguments:
- propagators: float32 [1024, 2, 128, 128], P(('grp', 'slot')), may hold values from -1 to 1, as said below
Outputs:
- forward: float32 [1024, 2, 128, 128], P(('grp', 'slot'))
The draws below stay inside these ranges and needn't reach their ends.
Inputs may be any that keep to these rules, and one draw needn't show every extreme that they name: `propagators`: each slice is a unitary matrix of order 128, given as real and imaginary parts.
All inputs are finite; a program needn't handle non-finite values.
Results may differ from the reference program's by a relative error of at most 0.0003.
Values sent between devices are 32-bit elements; how exact they have to be, the bound alone decides.
No kernel may reach another device: no remote copies, remote signals or barrier semaphores. Data moves between devices by JAX's collectives and lax.ppermute only.
A program may use at most 64 MiB of HBM per device.

```python
import math
import jax
import jax.numpy as jnp
from jax import lax

M = 128
TOTAL = 1024


def draw_propagators(key, part):
    strength = 1.0
    keys = jax.random.split(jax.random.fold_in(key, 17), TOTAL)

    def single(subkey):
        first, second = jax.random.split(subkey)
        raw_real = jax.random.normal(first, (M, M), jnp.float32)
        raw_imag = jax.random.normal(second, (M, M), jnp.float32)
        herm_real = (raw_real + raw_real.T) * (strength / (2.0 * M ** 0.5))
        herm_imag = (raw_imag - raw_imag.T) * (strength / (2.0 * M ** 0.5))
        identity = jnp.eye(M, dtype=jnp.float32)
        left_real = identity + herm_imag
        left_imag = -herm_real
        right_real = identity - herm_imag
        right_imag = herm_real
        system = jnp.block([[left_real, -left_imag], [left_imag, left_real]])
        target = jnp.concatenate([right_real, right_imag], axis=0)
        solved = jnp.linalg.solve(system, target)
        return jnp.stack([solved[:M], solved[M:]])
    return lax.map(single, keys).astype(jnp.float32)


def setup_inputs(seed: int = 0) -> dict:
    key_list = jax.random.split(jax.random.key(seed), 2)
    return {
        "propagators": draw_propagators(jax.random.fold_in(key_list[1], 71), 0),
    }


def complex_product(left, right):
    high = lax.Precision.HIGHEST
    real_part = jnp.dot(left[0], right[0], precision=high) - jnp.dot(left[1], right[1], precision=high)
    imag_part = jnp.dot(left[0], right[1], precision=high) + jnp.dot(left[1], right[0], precision=high)
    return jnp.stack([real_part, imag_part])

def reference(propagators):
    order = propagators.shape[2]
    identity = jnp.stack([jnp.eye(order, dtype=jnp.float32), jnp.zeros((order, order), jnp.float32)])

    def advance(running, unitary):
        updated = complex_product(unitary, running)
        return (updated, updated)
    final_value, prefixes = lax.scan(advance, identity.astype(propagators.dtype), propagators)
    return prefixes * math.sqrt(order)
```

```python
import functools
import math

import jax
import jax.numpy as jnp
import numpy as np
from jax import lax
from jax.experimental import pallas as pl
from jax.experimental.pallas import tpu as pltpu
from jax.sharding import Mesh, PartitionSpec as P

VMEM = pltpu.VMEM
F32 = jnp.float32

EIGHT = ([(0, 1), (2, 3), (4, 5), (6, 7)], [(1, 2), (0, 3), (5, 6), (4, 7)], [(0, 6), (1, 7), (2, 4), (3, 5)])
FOUR = ([(0, 1), (2, 3)], [(0, 3), (1, 2)])
LEVELS = [(2, EIGHT[i], i) for i in range(3)] + [(1, FOUR[i], 3 + i) for i in range(2)] + [(0, EIGHT[i], 5 + i) for i in range(3)]


def pairs_along(ids, axis, pairs):
    lines = np.moveaxis(ids, axis, -1).reshape(-1, ids.shape[axis])
    return [[int(line[a]), int(line[b])] for line in lines for a, b in pairs]


def split(x):
    high = x.astype(jnp.bfloat16)
    rest = x - high.astype(F32)
    mid = rest.astype(jnp.bfloat16)
    low = (rest - mid.astype(F32)).astype(jnp.bfloat16)
    return high, mid, low


def product(a, b):
    cat = jnp.concatenate
    left = [cat([cat([r, -i], 1), cat([i, r], 1)], 0) for r, i in zip(split(a[0]), split(a[1]))]
    right = [cat([r, i], 0) for r, i in zip(split(b[0]), split(b[1]))]
    dot = functools.partial(jnp.dot, preferred_element_type=F32)
    n = a[0].shape[1]
    both = cat(right[:2], 1)
    c0, c1 = dot(left[0], both), dot(left[1], both)
    small = dot(left[0], right[2]) + dot(left[2], right[0]) + c1[:, n:]
    c = small + (c0[:, n:] + c1[:, :n]) + c0[:, :n]
    return c[:n], c[n:]


def load(ref, *i):
    return ref[(*i, 0)], ref[(*i, 1)]


def store(ref, c, *i):
    ref[(*i, 0)] = c[0]
    ref[(*i, 1)] = c[1]


def begin(flag, u, total, inner):
    first = product(load(u, 0, 1), load(u, 0, 0))
    second = product(load(u, 1, 1), load(u, 1, 0))
    whole = product(second, first)
    store(total, whole)

    @pl.when(flag[0] == 0)
    def _():
        inner[0] = u[0, 0]
        store(inner, first, 1)

    @pl.when(flag[0] == 1)
    def _():
        store(inner, product(load(u, 1, 0), first), 0)
        store(inner, whole, 1)


def level(bit, first, last, flag, g, *refs):
    refs = list(refs)
    before = None if first else refs.pop(0)
    if not last:
        store(refs.pop(0), product(load(g, 1), load(g, 0)))
    after = refs.pop(0)
    upper = lax.rem(lax.div(flag[0], 2 << bit), 2) == 1

    @pl.when(upper)
    def _():
        if first:
            after[...] = g[0]
        else:
            store(after, product(load(before), load(g, 0)))

    @pl.when(jnp.logical_not(upper))
    def _():
        if first:
            n = g.shape[-1]
            one = lax.broadcasted_iota(jnp.int32, (n, n), 0) == lax.broadcasted_iota(jnp.int32, (n, n), 1)
            after[0] = jnp.where(one, 1.0, 0.0).astype(F32)
            after[1] = jnp.zeros((n, n), F32)
        else:
            after[...] = before[...]


def end(scale, inner, e, out):
    for j in range(2):
        c = product(load(inner, j), load(e, 1))
        store(out, (c[0] * scale, c[1] * scale), j)


def call(body, outs, *args):
    smem = pl.BlockSpec(memory_space=pltpu.SMEM)
    vmem = pl.BlockSpec(memory_space=VMEM)
    return pl.pallas_call(
        body,
        out_shape=outs,
        in_specs=[smem if a.dtype == jnp.int32 else vmem for a in args],
        out_specs=jax.tree.map(lambda _: vmem, outs),
        compiler_params=pltpu.CompilerParams(vmem_limit_bytes=16 << 20),
    )(*args)


def local(ids, u):
    n = u.shape[-1]
    scale = math.sqrt(n)
    one = jax.ShapeDtypeStruct((2, n, n), F32)
    two = jax.ShapeDtypeStruct((2, 2, n, n), F32)
    me = lax.axis_index("d").astype(jnp.int32)
    number = me.reshape(1)
    chip = [[int(a), int(b)] for a, b in ids.reshape(-1, 2)]
    both = lax.all_gather(u, "d", axis_index_groups=chip)
    total, inner = call(begin, (one, two), lax.rem(number, 2), both)
    e = None
    for k, (axis, pairs, bit) in enumerate(LEVELS):
        other = 0 if axis == 2 else 2
        groups = pairs_along(ids[..., 1], axis, pairs) + pairs_along(ids[..., 0], other, EIGHT[0])
        g = lax.all_gather(total, "d", axis_index_groups=groups)
        last = k == len(LEVELS) - 1
        body = functools.partial(level, bit, k == 0, last)
        args = (number, g) + (() if e is None else (e,))
        if last:
            (e,) = call(body, (one,), *args)
        else:
            total, e = call(body, (one, one), *args)
    e = lax.all_gather(e, "d", axis_index_groups=chip)
    return call(functools.partial(end, scale), (two,), inner, e)[0]


def solution(mesh):
    flat = Mesh(mesh.devices.reshape(-1), ("d",))
    ids = np.arange(flat.size).reshape(8, 4, 8, 2)
    return jax.shard_map(
        functools.partial(local, ids), mesh=flat, in_specs=(P("d"),), out_specs=P("d"), check_vma=False
    )
```

```python
import functools
import math

import jax
import jax.numpy as jnp
import numpy as np
from jax import lax
from jax.experimental import pallas as pl
from jax.experimental.pallas import tpu as pltpu
from jax.sharding import Mesh, PartitionSpec as P

F32 = jnp.float32
RING = ([(0, 1), (2, 3), (4, 5), (6, 7)], [(1, 2), (0, 3), (5, 6), (4, 7)], [(0, 7), (3, 4), (1, 6), (2, 5)])
SHORT = ([(0, 1), (2, 3)], [(0, 3), (1, 2)])


def groups_along(ids, axis, groups):
    out = []
    for core in (1, 0):
        lines = np.moveaxis(ids[..., core], axis, -1).reshape(-1, ids.shape[axis])
        out += [[int(line[i]) for i in g] for line in lines for g in groups]
    return out


def split(x):
    high = x.astype(jnp.bfloat16)
    rest = x - high.astype(F32)
    mid = rest.astype(jnp.bfloat16)
    low = (rest - mid.astype(F32)).astype(jnp.bfloat16)
    return high, mid, low


def times(lefts, right):
    cat = jnp.concatenate
    n = right[0].shape[0]
    a = split(cat([cat(left, 1) for left in lefts], 0))
    b = [cat([cat([r, i], 1), cat([-i, r], 1)], 0) for r, i in zip(split(right[0]), split(right[1]))]
    dot = functools.partial(jnp.dot, preferred_element_type=F32)
    c = dot(a[0], b[2]) + dot(a[2], b[0]) + dot(a[1], b[1])
    c = c + (dot(a[0], b[1]) + dot(a[1], b[0])) + dot(a[0], b[0])
    return [(c[k * n : (k + 1) * n, :n], c[k * n : (k + 1) * n, n:]) for k in range(len(lefts))]


def load(ref, *i):
    return ref[(*i, 0)], ref[(*i, 1)]


def store(ref, c, *i):
    ref[(*i, 0)] = c[0]
    ref[(*i, 1)] = c[1]


def where(flag, a, b):
    return tuple(jnp.where(flag, x, y) for x, y in zip(a, b))


def begin(core, u, total, inner):
    (first,) = times([load(u, 0, 1)], load(u, 0, 0))
    (second,) = times([load(u, 1, 1)], load(u, 1, 0))
    whole, third = times([second, load(u, 1, 0)], first)
    store(total, whole)
    one = core[0] == 1
    store(inner, where(one, third, load(u, 0, 0)), 0)
    store(inner, where(one, whole, first), 1)


def pair_first(upper, g, total, after):
    (whole,) = times([load(g, 1)], load(g, 0))
    store(total, whole)
    n = g.shape[-1]
    eye = lax.broadcasted_iota(jnp.int32, (n, n), 0) == lax.broadcasted_iota(jnp.int32, (n, n), 1)
    one = jnp.where(eye, 1.0, 0.0).astype(F32), jnp.zeros((n, n), F32)
    store(after, where(upper[0] == 1, load(g, 0), one))


def pair(upper, g, before, total, after):
    e = load(before)
    whole, more = times([load(g, 1), e], load(g, 0))
    store(total, whole)
    store(after, where(upper[0] == 1, more, e))


def pair_last(upper, g, before, after):
    e = load(before)
    (more,) = times([e], load(g, 0))
    store(after, where(upper[0] == 1, more, e))


def end(scale, inner, e, out):
    for j, c in enumerate(times([load(inner, 0), load(inner, 1)], load(e))):
        store(out, (c[0] * scale, c[1] * scale), j)


def call(body, outs, *args):
    smem = pl.BlockSpec(memory_space=pltpu.SMEM)
    vmem = pl.BlockSpec(memory_space=pltpu.VMEM)
    return pl.pallas_call(
        body,
        out_shape=outs,
        in_specs=[smem if a.dtype == jnp.int32 else vmem for a in args],
        out_specs=jax.tree.map(lambda _: vmem, outs),
        compiler_params=pltpu.CompilerParams(vmem_limit_bytes=16 << 20),
    )(*args)


def local(ids, u):
    n = u.shape[-1]
    one = jax.ShapeDtypeStruct((2, n, n), F32)
    two = jax.ShapeDtypeStruct((2, 2, n, n), F32)
    me = lax.axis_index("d").astype(jnp.uint32)
    core, z, x, y = me % 2, me // 2 % 8, me // 16 % 4, me // 64
    chip = [[int(a), int(b)] for a, b in ids.reshape(-1, 2)]
    flag = lambda value: value.astype(jnp.int32).reshape(1)

    def gather(value, axis, groups):
        return lax.all_gather(value, "d", axis_index_groups=groups_along(ids, axis, groups))

    def tree(total):
        total, e = call(pair_first, (one, one), flag(z % 2), gather(total, 2, RING[0]))
        for axis, place, level in ((2, z // 2, RING[1]), (2, z // 4, RING[2]), (1, x, SHORT[0]), (1, x // 2, SHORT[1]), (0, y, RING[0]), (0, y // 2, RING[1])):
            total, e = call(pair, (one, one), flag(place % 2), gather(total, axis, level), e)
        return call(pair_last, one, flag(y // 4), gather(total, 0, RING[2]), e)

    def from_core_one(e):
        return lax.all_gather(e, "d", axis_index_groups=chip)[1]

    def nothing_before(e):
        eye = jnp.eye(n, dtype=F32)
        return jnp.stack([eye, jnp.zeros_like(eye)])

    both = lax.all_gather(u, "d", axis_index_groups=chip)
    total, inner = call(begin, (one, two), flag(core), both)
    e = lax.cond(core == 1, tree, lambda total: total, total)
    e = lax.cond(me < 2, nothing_before, from_core_one, e)
    return call(functools.partial(end, math.sqrt(n)), two, inner, e)


def solution(mesh):
    flat = Mesh(mesh.devices.reshape(-1), ("d",))
    ids = np.arange(flat.size).reshape(8, 4, 8, 2)
    return jax.shard_map(
        functools.partial(local, ids), mesh=flat, in_specs=(P("d"),), out_specs=P("d"), check_vma=False
    )
```

```python
import functools
import math

import jax
import jax.numpy as jnp
import numpy as np
from jax import lax
from jax.experimental import pallas as pl
from jax.experimental.pallas import tpu as pltpu
from jax.sharding import Mesh, PartitionSpec as P

F32 = jnp.float32
LAST = [(0, 7), (3, 4), (1, 6), (2, 5)]
RING = ([(0, 1), (2, 3), (4, 5), (6, 7)], [(1, 2), (0, 3), (5, 6), (4, 7)], [(0, 6), (1, 7), (2, 4), (3, 5)])
SHORT = ([(0, 1), (2, 3)], [(0, 3), (1, 2)])


def groups_along(ids, axis, groups):
    out = []
    for core in (1, 0):
        lines = np.moveaxis(ids[..., core], axis, -1).reshape(-1, ids.shape[axis])
        out += [[int(line[i]) for i in g] for line in lines for g in groups]
    return out


def split(x):
    high = x.astype(jnp.bfloat16)
    rest = x - high.astype(F32)
    mid = rest.astype(jnp.bfloat16)
    low = (rest - mid.astype(F32)).astype(jnp.bfloat16)
    return high, mid, low


def times(lefts, right, exact=None):
    cat = jnp.concatenate
    n = right[0].shape[0]
    rows = n * (len(lefts) if exact is None else exact)
    a = split(cat([cat(left, 1) for left in lefts], 0))
    b = [cat([cat([r, i], 1), cat([-i, r], 1)], 0) for r, i in zip(split(right[0]), split(right[1]))]
    dot = functools.partial(jnp.dot, preferred_element_type=F32)
    c = dot(a[0], b[1]) + dot(a[1], b[0])
    if rows:
        more = dot(a[0][:rows], b[2]) + dot(a[2][:rows], b[0]) + dot(a[1][:rows], b[1])
        c = c + more if rows == c.shape[0] else cat([c[:rows] + more, c[rows:]], 0)
    c = c + dot(a[0], b[0])
    return [(c[k * n : (k + 1) * n, :n], c[k * n : (k + 1) * n, n:]) for k in range(len(lefts))]


def load(ref, *i):
    return ref[(*i, 0)], ref[(*i, 1)]


def store(ref, c, *i):
    ref[(*i, 0)] = c[0]
    ref[(*i, 1)] = c[1]


def where(flag, a, b):
    return tuple(jnp.where(flag, x, y) for x, y in zip(a, b))


def begin(core, u, total, inner):
    (first,) = times([load(u, 0, 1)], load(u, 0, 0))
    (second,) = times([load(u, 1, 1)], load(u, 1, 0))
    whole, third = times([second, load(u, 1, 0)], first)
    store(total, whole)
    one = core[0] == 1
    store(inner, where(one, third, load(u, 0, 0)), 0)
    store(inner, where(one, whole, first), 1)


def pair_first(upper, g, total, after):
    (whole,) = times([load(g, 1)], load(g, 0))
    store(total, whole)
    n = g.shape[-1]
    eye = lax.broadcasted_iota(jnp.int32, (n, n), 0) == lax.broadcasted_iota(jnp.int32, (n, n), 1)
    one = jnp.where(eye, 1.0, 0.0).astype(F32), jnp.zeros((n, n), F32)
    store(after, where(upper[0] == 1, load(g, 0), one))


def pair(upper, g, before, total, after):
    e = load(before)
    whole, more = times([load(g, 1), e], load(g, 0), 1)
    store(total, whole)
    store(after, where(upper[0] == 1, more, e))


def pair_last(upper, g, before, after):
    e = load(before)
    (more,) = times([e], load(g, 0), 0)
    store(after, where(upper[0] == 1, more, e))


def end(scale, inner, e, out):
    for j, c in enumerate(times([load(inner, 0), load(inner, 1)], load(e), 0)):
        store(out, (c[0] * scale, c[1] * scale), j)


def call(body, outs, *args):
    smem = pl.BlockSpec(memory_space=pltpu.SMEM)
    vmem = pl.BlockSpec(memory_space=pltpu.VMEM)
    return pl.pallas_call(
        body,
        out_shape=outs,
        in_specs=[smem if a.dtype == jnp.int32 else vmem for a in args],
        out_specs=jax.tree.map(lambda _: vmem, outs),
        compiler_params=pltpu.CompilerParams(vmem_limit_bytes=16 << 20),
    )(*args)


def local(ids, u):
    n = u.shape[-1]
    one = jax.ShapeDtypeStruct((2, n, n), F32)
    two = jax.ShapeDtypeStruct((2, 2, n, n), F32)
    me = lax.axis_index("d").astype(jnp.uint32)
    core, z, x, y = me % 2, me // 2 % 8, me // 16 % 4, me // 64
    chip = [[int(a), int(b)] for a, b in ids.reshape(-1, 2)]
    flag = lambda value: value.astype(jnp.int32).reshape(1)

    def gather(value, axis, groups):
        return lax.all_gather(value, "d", axis_index_groups=groups_along(ids, axis, groups))

    def tree(total):
        total, e = call(pair_first, (one, one), flag(z % 2), gather(total, 2, RING[0]))
        for axis, place, level in ((2, z // 2, RING[1]), (2, z // 4, RING[2]), (1, x, SHORT[0]), (1, x // 2, SHORT[1]), (0, y, RING[0]), (0, y // 2, RING[1])):
            total, e = call(pair, (one, one), flag(place % 2), gather(total, axis, level), e)
        return call(pair_last, one, flag(y // 4), gather(total, 0, LAST), e)

    def from_core_one(e):
        return lax.all_gather(e, "d", axis_index_groups=chip)[1]

    def nothing_before(e):
        eye = jnp.eye(n, dtype=F32)
        return jnp.stack([eye, jnp.zeros_like(eye)])

    both = lax.all_gather(u, "d", axis_index_groups=chip)
    total, inner = call(begin, (one, two), flag(core), both)
    e = lax.cond(core == 1, tree, lambda total: total, total)
    e = lax.cond(me < 2, nothing_before, from_core_one, e)
    return call(functools.partial(end, math.sqrt(n)), two, inner, e)


def solution(mesh):
    flat = Mesh(mesh.devices.reshape(-1), ("d",))
    ids = np.arange(flat.size).reshape(8, 4, 8, 2)
    return jax.shard_map(
        functools.partial(local, ids), mesh=flat, in_specs=(P("d"),), out_specs=P("d"), check_vma=False
    )
```

```python
import functools
import math

import jax
import jax.numpy as jnp
import numpy as np
from jax import lax
from jax.experimental import pallas as pl
from jax.experimental.pallas import tpu as pltpu
from jax.sharding import Mesh, PartitionSpec as P

F32 = jnp.float32
LAST = [(0, 7), (3, 4), (1, 6), (2, 5)]
RING = ([(0, 1), (2, 3), (4, 5), (6, 7)], [(1, 2), (0, 3), (5, 6), (4, 7)], [(0, 6), (1, 7), (2, 4), (3, 5)])
SHORT = ([(0, 1), (2, 3)], [(0, 3), (1, 2)])


def groups_along(ids, axis, groups):
    out = []
    for core in (1, 0):
        lines = np.moveaxis(ids[..., core], axis, -1).reshape(-1, ids.shape[axis])
        out += [[int(line[i]) for i in g] for line in lines for g in groups]
    return out


def split(x):
    high = x.astype(jnp.bfloat16)
    rest = x - high.astype(F32)
    mid = rest.astype(jnp.bfloat16)
    low = (rest - mid.astype(F32)).astype(jnp.bfloat16)
    return high, mid, low


def times(lefts, right, exact=None):
    cat = jnp.concatenate
    n = right[0].shape[0]
    rows = n * (len(lefts) if exact is None else exact)
    a = split(cat([cat(left, 1) for left in lefts], 0))
    b = [cat([cat([r, i], 1), cat([-i, r], 1)], 0) for r, i in zip(split(right[0]), split(right[1]))]
    dot = functools.partial(jnp.dot, preferred_element_type=F32)
    c = dot(a[0], b[1]) + dot(a[1], b[0])
    if rows:
        more = dot(a[0][:rows], b[2]) + dot(a[2][:rows], b[0]) + dot(a[1][:rows], b[1])
        c = c + more if rows == c.shape[0] else cat([c[:rows] + more, c[rows:]], 0)
    c = c + dot(a[0], b[0])
    return [(c[k * n : (k + 1) * n, :n], c[k * n : (k + 1) * n, n:]) for k in range(len(lefts))]


def load(ref, *i):
    return ref[(*i, 0)], ref[(*i, 1)]


def store(ref, c, *i):
    ref[(*i, 0)] = c[0]
    ref[(*i, 1)] = c[1]


def where(flag, a, b):
    return tuple(jnp.where(flag, x, y) for x, y in zip(a, b))


def begin(core, u, total, inner):
    (first,) = times([load(u, 0, 1)], load(u, 0, 0))
    (second,) = times([load(u, 1, 1)], load(u, 1, 0))
    whole, third = times([second, load(u, 1, 0)], first, 1)
    store(total, whole)
    one = core[0] == 1
    store(inner, where(one, third, load(u, 0, 0)), 0)
    store(inner, where(one, whole, first), 1)


def pair_first(upper, g, total, after):
    (whole,) = times([load(g, 1)], load(g, 0))
    store(total, whole)
    n = g.shape[-1]
    eye = lax.broadcasted_iota(jnp.int32, (n, n), 0) == lax.broadcasted_iota(jnp.int32, (n, n), 1)
    one = jnp.where(eye, 1.0, 0.0).astype(F32), jnp.zeros((n, n), F32)
    store(after, where(upper[0] == 1, load(g, 0), one))


def pair(exact, upper, g, before, total, after):
    e = load(before)
    whole, more = times([load(g, 1), e], load(g, 0), exact)
    store(total, whole)
    store(after, where(upper[0] == 1, more, e))


def pair_last(upper, g, before, after):
    e = load(before)
    (more,) = times([e], load(g, 0), 0)
    store(after, where(upper[0] == 1, more, e))


def end(scale, inner, e, out):
    for j, c in enumerate(times([load(inner, 0), load(inner, 1)], load(e), 0)):
        store(out, (c[0] * scale, c[1] * scale), j)


def call(body, outs, *args):
    smem = pl.BlockSpec(memory_space=pltpu.SMEM)
    vmem = pl.BlockSpec(memory_space=pltpu.VMEM)
    return pl.pallas_call(
        body,
        out_shape=outs,
        in_specs=[smem if a.dtype == jnp.int32 else vmem for a in args],
        out_specs=jax.tree.map(lambda _: vmem, outs),
        compiler_params=pltpu.CompilerParams(vmem_limit_bytes=16 << 20),
    )(*args)


def local(ids, u):
    n = u.shape[-1]
    one = jax.ShapeDtypeStruct((2, n, n), F32)
    two = jax.ShapeDtypeStruct((2, 2, n, n), F32)
    me = lax.axis_index("d").astype(jnp.uint32)
    core, z, x, y = me % 2, me // 2 % 8, me // 16 % 4, me // 64
    chip = [[int(a), int(b)] for a, b in ids.reshape(-1, 2)]
    flag = lambda value: value.astype(jnp.int32).reshape(1)

    def gather(value, axis, groups):
        return lax.all_gather(value, "d", axis_index_groups=groups_along(ids, axis, groups))

    def tree(total):
        total, e = call(pair_first, (one, one), flag(z % 2), gather(total, 2, RING[0]))
        for axis, place, level in ((2, z // 2, RING[1]), (2, z // 4, RING[2]), (1, x, SHORT[0]), (1, x // 2, SHORT[1]), (0, y, RING[0]), (0, y // 2, RING[1])):
            total, e = call(functools.partial(pair, int(axis != 0)), (one, one), flag(place % 2), gather(total, axis, level), e)
        return call(pair_last, one, flag(y // 4), gather(total, 0, LAST), e)

    def from_core_one(e):
        return lax.all_gather(e, "d", axis_index_groups=chip)[1]

    def nothing_before(e):
        eye = jnp.eye(n, dtype=F32)
        return jnp.stack([eye, jnp.zeros_like(eye)])

    both = lax.all_gather(u, "d", axis_index_groups=chip)
    total, inner = call(begin, (one, two), flag(core), both)
    e = lax.cond(core == 1, tree, lambda total: total, total)
    e = lax.cond(me < 2, nothing_before, from_core_one, e)
    return call(functools.partial(end, math.sqrt(n)), two, inner, e)


def solution(mesh):
    flat = Mesh(mesh.devices.reshape(-1), ("d",))
    ids = np.arange(flat.size).reshape(8, 4, 8, 2)
    return jax.shard_map(
        functools.partial(local, ids), mesh=flat, in_specs=(P("d"),), out_specs=P("d"), check_vma=False
    )
```

```python
import functools
import math

import jax
import jax.numpy as jnp
import numpy as np
from jax import lax
from jax.experimental import pallas as pl
from jax.experimental.pallas import tpu as pltpu
from jax.sharding import Mesh, PartitionSpec as P

F32 = jnp.float32
LAST = [(0, 7), (3, 4), (1, 6), (2, 5)]
RING = ([(0, 1), (2, 3), (4, 5), (6, 7)], [(1, 2), (0, 3), (5, 6), (4, 7)], [(0, 6), (1, 7), (2, 4), (3, 5)])
SHORT = ([(0, 1), (2, 3)], [(0, 3), (1, 2)])


def groups_along(ids, axis, groups):
    out = []
    for core in (1, 0):
        lines = np.moveaxis(ids[..., core], axis, -1).reshape(-1, ids.shape[axis])
        out += [[int(line[i]) for i in g] for line in lines for g in groups]
    return out


def split(x):
    high = x.astype(jnp.bfloat16)
    rest = x - high.astype(F32)
    mid = rest.astype(jnp.bfloat16)
    low = (rest - mid.astype(F32)).astype(jnp.bfloat16)
    return high, mid, low


def times(lefts, right, exact=None):
    cat = jnp.concatenate
    n = right[0].shape[0]
    rows = n * (len(lefts) if exact is None else exact)
    a = split(cat([cat(left, 1) for left in lefts], 0))
    b = [cat([cat([r, i], 1), cat([-i, r], 1)], 0) for r, i in zip(split(right[0]), split(right[1]))]
    dot = functools.partial(jnp.dot, preferred_element_type=F32)
    c = dot(a[0], b[1]) + dot(a[1], b[0])
    if rows:
        more = dot(a[0][:rows], b[2]) + dot(a[2][:rows], b[0]) + dot(a[1][:rows], b[1])
        c = c + more if rows == c.shape[0] else cat([c[:rows] + more, c[rows:]], 0)
    c = c + dot(a[0], b[0])
    return [(c[k * n : (k + 1) * n, :n], c[k * n : (k + 1) * n, n:]) for k in range(len(lefts))]


def load(ref, *i):
    return ref[(*i, 0)], ref[(*i, 1)]


def store(ref, c, *i):
    ref[(*i, 0)] = c[0]
    ref[(*i, 1)] = c[1]


def where(flag, a, b):
    return tuple(jnp.where(flag, x, y) for x, y in zip(a, b))


def begin(core, u, total, inner):
    (first,) = times([load(u, 0, 1)], load(u, 0, 0))
    (second,) = times([load(u, 1, 1)], load(u, 1, 0))
    whole, third = times([second, load(u, 1, 0)], first, 1)
    store(total, whole)
    one = core[0] == 1
    store(inner, where(one, third, load(u, 0, 0)), 0)
    store(inner, where(one, whole, first), 1)


def pair_first(upper, g, total, after):
    (whole,) = times([load(g, 1)], load(g, 0))
    store(total, whole)
    n = g.shape[-1]
    eye = lax.broadcasted_iota(jnp.int32, (n, n), 0) == lax.broadcasted_iota(jnp.int32, (n, n), 1)
    one = jnp.where(eye, 1.0, 0.0).astype(F32), jnp.zeros((n, n), F32)
    store(after, where(upper[0] == 1, load(g, 0), one))


def pair(exact, upper, g, before, total, after):
    e = load(before)
    whole, more = times([load(g, 1), e], load(g, 0), exact)
    store(total, whole)
    store(after, where(upper[0] == 1, more, e))


def pair_last(upper, g, before, after):
    @pl.when(upper[0] == 1)
    def _():
        store(after, times([load(before)], load(g, 0), 0)[0])

    @pl.when(upper[0] == 0)
    def _():
        after[...] = before[...]


def end(scale, inner, e, out):
    for j, c in enumerate(times([load(inner, 0), load(inner, 1)], load(e), 0)):
        store(out, (c[0] * scale, c[1] * scale), j)


def call(body, outs, *args):
    smem = pl.BlockSpec(memory_space=pltpu.SMEM)
    vmem = pl.BlockSpec(memory_space=pltpu.VMEM)
    return pl.pallas_call(
        body,
        out_shape=outs,
        in_specs=[smem if a.dtype == jnp.int32 else vmem for a in args],
        out_specs=jax.tree.map(lambda _: vmem, outs),
        compiler_params=pltpu.CompilerParams(vmem_limit_bytes=16 << 20),
    )(*args)


def local(ids, u):
    n = u.shape[-1]
    one = jax.ShapeDtypeStruct((2, n, n), F32)
    two = jax.ShapeDtypeStruct((2, 2, n, n), F32)
    me = lax.axis_index("d").astype(jnp.uint32)
    core, z, x, y = me % 2, me // 2 % 8, me // 16 % 4, me // 64
    chip = [[int(a), int(b)] for a, b in ids.reshape(-1, 2)]
    flag = lambda value: value.astype(jnp.int32).reshape(1)

    def gather(value, axis, groups):
        return lax.all_gather(value, "d", axis_index_groups=groups_along(ids, axis, groups))

    def tree(total):
        total, e = call(pair_first, (one, one), flag(z % 2), gather(total, 2, RING[0]))
        for axis, place, level in ((2, z // 2, RING[1]), (2, z // 4, RING[2]), (1, x, SHORT[0]), (1, x // 2, SHORT[1]), (0, y, RING[0]), (0, y // 2, RING[1])):
            total, e = call(functools.partial(pair, int(axis != 0)), (one, one), flag(place % 2), gather(total, axis, level), e)
        return call(pair_last, one, flag(y // 4), gather(total, 0, LAST), e)

    def from_core_one(e):
        return lax.all_gather(e, "d", axis_index_groups=chip)[1]

    def nothing_before(e):
        eye = jnp.eye(n, dtype=F32)
        return jnp.stack([eye, jnp.zeros_like(eye)])

    both = lax.all_gather(u, "d", axis_index_groups=chip)
    total, inner = call(begin, (one, two), flag(core), both)
    e = lax.cond(core == 1, tree, lambda total: total, total)
    e = lax.cond(me < 2, nothing_before, from_core_one, e)
    return call(functools.partial(end, math.sqrt(n)), two, inner, e)


def solution(mesh):
    flat = Mesh(mesh.devices.reshape(-1), ("d",))
    ids = np.arange(flat.size).reshape(8, 4, 8, 2)
    return jax.shard_map(
        functools.partial(local, ids), mesh=flat, in_specs=(P("d"),), out_specs=P("d"), check_vma=False
    )
```

```python
import functools
import math

import jax
import jax.numpy as jnp
import numpy as np
from jax import lax
from jax.experimental import pallas as pl
from jax.experimental.pallas import tpu as pltpu
from jax.sharding import Mesh, PartitionSpec as P

F32 = jnp.float32
LAST = [(0, 7), (3, 4), (1, 6), (2, 5)]
RING = ([(0, 1), (2, 3), (4, 5), (6, 7)], [(1, 2), (0, 3), (5, 6), (4, 7)], [(0, 6), (1, 7), (2, 4), (3, 5)])
SHORT = ([(0, 1), (2, 3)], [(0, 3), (1, 2)])


def groups_along(ids, axis, groups):
    out = []
    for core in (1, 0):
        lines = np.moveaxis(ids[..., core], axis, -1).reshape(-1, ids.shape[axis])
        out += [[int(line[i]) for i in g] for line in lines for g in groups]
    return out


def split(x):
    high = x.astype(jnp.bfloat16)
    rest = x - high.astype(F32)
    mid = rest.astype(jnp.bfloat16)
    low = (rest - mid.astype(F32)).astype(jnp.bfloat16)
    return high, mid, low


def times(lefts, right, exact=None):
    cat = jnp.concatenate
    n = right[0].shape[0]
    rows = n * (len(lefts) if exact is None else exact)
    a = split(cat([cat(left, 1) for left in lefts], 0))
    b = [cat([cat([r, i], 1), cat([-i, r], 1)], 0) for r, i in zip(split(right[0]), split(right[1]))]
    dot = functools.partial(jnp.dot, preferred_element_type=F32)
    c = dot(a[0], b[1]) + dot(a[1], b[0])
    if rows:
        more = dot(a[0][:rows], b[2]) + dot(a[2][:rows], b[0]) + dot(a[1][:rows], b[1])
        c = c + more if rows == c.shape[0] else cat([c[:rows] + more, c[rows:]], 0)
    c = c + dot(a[0], b[0])
    return [(c[k * n : (k + 1) * n, :n], c[k * n : (k + 1) * n, n:]) for k in range(len(lefts))]


def load(ref, *i):
    return ref[(*i, 0)], ref[(*i, 1)]


def store(ref, c, *i):
    ref[(*i, 0)] = c[0]
    ref[(*i, 1)] = c[1]


def where(flag, a, b):
    return tuple(jnp.where(flag, x, y) for x, y in zip(a, b))


def begin(core, u, total, inner):
    (first,) = times([load(u, 0, 1)], load(u, 0, 0))
    (second,) = times([load(u, 1, 1)], load(u, 1, 0))
    whole, third = times([second, load(u, 1, 0)], first, 1)
    store(total, whole)
    one = core[0] == 1
    store(inner, where(one, third, load(u, 0, 0)), 0)
    store(inner, where(one, whole, first), 1)


def pair_first(upper, g, total, after):
    (whole,) = times([load(g, 1)], load(g, 0))
    store(total, whole)
    n = g.shape[-1]
    eye = lax.broadcasted_iota(jnp.int32, (n, n), 0) == lax.broadcasted_iota(jnp.int32, (n, n), 1)
    one = jnp.where(eye, 1.0, 0.0).astype(F32), jnp.zeros((n, n), F32)
    store(after, where(upper[0] == 1, load(g, 0), one))


def pair(exact, upper, g, before, total, after):
    @pl.when(upper[0] == 1)
    def _():
        whole, more = times([load(g, 1), load(before)], load(g, 0), exact)
        store(total, whole)
        store(after, more)

    @pl.when(upper[0] == 0)
    def _():
        store(total, times([load(g, 1)], load(g, 0), exact)[0])
        after[...] = before[...]


def pair_last(upper, g, before, after):
    @pl.when(upper[0] == 1)
    def _():
        store(after, times([load(before)], load(g, 0), 0)[0])

    @pl.when(upper[0] == 0)
    def _():
        after[...] = before[...]


def end(scale, inner, e, out):
    for j, c in enumerate(times([load(inner, 0), load(inner, 1)], load(e), 0)):
        store(out, (c[0] * scale, c[1] * scale), j)


def call(body, outs, *args):
    smem = pl.BlockSpec(memory_space=pltpu.SMEM)
    vmem = pl.BlockSpec(memory_space=pltpu.VMEM)
    return pl.pallas_call(
        body,
        out_shape=outs,
        in_specs=[smem if a.dtype == jnp.int32 else vmem for a in args],
        out_specs=jax.tree.map(lambda _: vmem, outs),
        compiler_params=pltpu.CompilerParams(vmem_limit_bytes=16 << 20),
    )(*args)


def local(ids, u):
    n = u.shape[-1]
    one = jax.ShapeDtypeStruct((2, n, n), F32)
    two = jax.ShapeDtypeStruct((2, 2, n, n), F32)
    me = lax.axis_index("d").astype(jnp.uint32)
    core, z, x, y = me % 2, me // 2 % 8, me // 16 % 4, me // 64
    chip = [[int(a), int(b)] for a, b in ids.reshape(-1, 2)]
    flag = lambda value: value.astype(jnp.int32).reshape(1)

    def gather(value, axis, groups):
        return lax.all_gather(value, "d", axis_index_groups=groups_along(ids, axis, groups))

    def tree(total):
        total, e = call(pair_first, (one, one), flag(z % 2), gather(total, 2, RING[0]))
        for axis, place, level in ((2, z // 2, RING[1]), (2, z // 4, RING[2]), (1, x, SHORT[0]), (1, x // 2, SHORT[1]), (0, y, RING[0]), (0, y // 2, RING[1])):
            total, e = call(functools.partial(pair, int(axis != 0)), (one, one), flag(place % 2), gather(total, axis, level), e)
        return call(pair_last, one, flag(y // 4), gather(total, 0, LAST), e)

    def from_core_one(e):
        return lax.all_gather(e, "d", axis_index_groups=chip)[1]

    def nothing_before(e):
        eye = jnp.eye(n, dtype=F32)
        return jnp.stack([eye, jnp.zeros_like(eye)])

    both = lax.all_gather(u, "d", axis_index_groups=chip)
    total, inner = call(begin, (one, two), flag(core), both)
    e = lax.cond(core == 1, tree, lambda total: total, total)
    e = lax.cond(me < 2, nothing_before, from_core_one, e)
    return call(functools.partial(end, math.sqrt(n)), two, inner, e)


def solution(mesh):
    flat = Mesh(mesh.devices.reshape(-1), ("d",))
    ids = np.arange(flat.size).reshape(8, 4, 8, 2)
    return jax.shard_map(
        functools.partial(local, ids), mesh=flat, in_specs=(P("d"),), out_specs=P("d"), check_vma=False
    )
```
